32 devices in a mesh: grp: 2 (over y), sx: 4 (over z), sy: 4 (over x, core).
Axes of the slice: x: 2, y: 2, z: 4, core: 2. Of those that a mesh axis runs over, the one named last changes fastest.
Arguments:
- field: float32 [4, 128, 96, 128], P('grp', 'sx', 'sy'), parts along dimension 0, may hold values from -6 to 6
- factor_x: float32 [128, 96], P('sx'), may hold values from -0.75 to 0.75
- factor_y: float32 [96, 64], P('sy'), may hold values from -0.875 to 0.875
- factor_z: float32 [128, 32], replicated, may hold values from -0.75 to 0.75
Outputs:
- core: float32 [4, 96, 2048], P('grp', None, ('sx', 'sy')), parts along dimension 0
- residual: float32 [4, 128, 96, 128], P('grp', 'sx', 'sy'), parts along dimension 0
The draws below stay inside these ranges and needn't reach their ends.
There are 2 independent parts, one for each index of `grp`. The reference program is written for one: setup_inputs(seed, part) draws one part's arguments, and reference() takes and returns one part's arrays. A program takes and returns all parts, laid end to end along the dimension named above; an argument that names none is the same for every part. Nothing has to cross between parts.
All inputs are finite; a program needn't handle non-finite values.
Results may differ from the reference program's by a relative error of at most 0.000071.
Values sent between devices are 32-bit elements; how exact they have to be, the bound alone decides.
A program may use at most 64 MiB of HBM per device.

```python
import jax
import jax.numpy as jnp
from jax import lax

S = 2
NZ = 128
R1 = 96
R2 = 64
R3 = 32
NX = 128
NY = 96


def shard_levels(key, dims, split, smallest, top_value):
    loudness, own = 1.0, jax.random.fold_in(key, 6)
    for axis_at, parts in split:
        heights = jnp.exp(jax.random.uniform(jax.random.fold_in(own, axis_at), (parts,), jnp.float32, smallest / len(split), top_value / len(split)))
        loudness = loudness * jnp.repeat(heights, dims[axis_at] // parts).reshape([-1 if axis == axis_at else 1 for axis in range(len(dims))])
    return loudness


def centred(key, shape, width, bound, cuts=(), kind=jnp.bfloat16):
    factor_of = shard_levels(key, shape, cuts, -0.22, 0.18) if cuts else 1.0
    values = jax.random.normal(key, shape, jnp.float32) * width * factor_of
    return jnp.minimum(jnp.maximum(values, -bound), bound).astype(kind)


def setup_inputs(seed: int = 0, part: int = 0) -> dict:
    splits = jax.random.split(jax.random.key(seed), 5)
    own_keys = jax.random.split(jax.random.fold_in(splits[4], part), 5)
    return {
        "field": centred(own_keys[0], (S, NX, NY, NZ), 1.0, 6.0, ((1, 4), (2, 4)), jnp.float32),
        "factor_x": centred(splits[1], (NX, R1), (NX // 2) ** -0.5, 0.75, ((0, 4),), jnp.float32),
        "factor_y": centred(splits[2], (NY, R2), (NY // 2) ** -0.5, 0.875, ((0, 4),), jnp.float32),
        "factor_z": centred(splits[3], (NZ, R3), (NZ // 2) ** -0.5, 0.75, (), jnp.float32),
    }


def reference(field, factor_x, factor_y, factor_z):
    highest = lax.Precision.HIGHEST

    def project(snapshot):
        inner = jnp.einsum('xyz,zc->xyc', snapshot, factor_z, precision=highest)
        inner = jnp.einsum('xyc,yb->xbc', inner, factor_y, precision=highest)
        return jnp.einsum('xbc,xa->abc', inner, factor_x, precision=highest)

    core = lax.map(project, field)

    def rebuild(pair):
        snapshot, kernel = pair
        outer = jnp.einsum('abc,xa->xbc', kernel, factor_x, precision=highest)
        outer = jnp.einsum('xbc,yb->xyc', outer, factor_y, precision=highest)
        outer = jnp.einsum('xyc,zc->xyz', outer, factor_z, precision=highest)
        return snapshot - outer

    residual = lax.map(rebuild, (field, core))
    return core.reshape(S, R1, R2 * R3), residual
```

```python
import functools

import jax
import jax.numpy as jnp
from jax import lax
from jax.experimental import pallas as pl
from jax.experimental.pallas import tpu as pltpu
from jax.sharding import PartitionSpec as P

MESH = pl.DeviceIdType.MESH
F32 = jnp.float32
BF16 = jnp.bfloat16
NN = (((1,), (0,)), ((), ()))
NT = (((1,), (1,)), ((), ()))
TN = (((0,), (0,)), ((), ()))


def split(a):
    high = a.astype(BF16)
    return high, (a - high.astype(F32)).astype(BF16)


def dot(a, b, dims=NN):
    return lax.dot_general(a, b, dims, preferred_element_type=F32)


def dot3(a, b, dims=NN):
    return dot(a[0], b[0], dims) + (dot(a[0], b[1], dims) + dot(a[1], b[0], dims))


def iota(shape, axis):
    return lax.broadcasted_iota(jnp.int32, shape, axis)


def exchange_segments(tiles):
    segment = iota(tiles[0].shape, 1) // 32
    a, b, c, d = tiles
    low = segment < 2
    a, c = jnp.where(low, a, pltpu.roll(c, 64, 1)), jnp.where(low, pltpu.roll(a, 64, 1), c)
    b, d = jnp.where(low, b, pltpu.roll(d, 64, 1)), jnp.where(low, pltpu.roll(b, 64, 1), d)
    even = segment % 2 == 0
    a, b = jnp.where(even, a, pltpu.roll(b, 32, 1)), jnp.where(even, pltpu.roll(a, 96, 1), b)
    c, d = jnp.where(even, c, pltpu.roll(d, 32, 1)), jnp.where(even, pltpu.roll(c, 96, 1), d)
    return a, b, c, d


def kernel(nsx, nsy, field, fx, fy, fz, core_out, res_out, ux, uy, bd_h, bd_l, send1, recv1, send2, recv2,
           csend, crecv, ux_s, ux_r, uy_s, uy_r, s1_s, s1_r, s2_s, s2_r, c_s, c_r):
    n = nsx * nsy
    snaps, xl, yl, nz = field.shape
    sx, sy = lax.axis_index("sx"), lax.axis_index("sy")
    me = sx * nsy + sy

    def peer(i):
        q = lax.rem(me + i, n)
        return q, {"sx": q // nsy, "sy": lax.rem(q, nsy)}

    def send(src, dst, send_sems, recv_sems, i, device):
        return pltpu.make_async_remote_copy(src_ref=src, dst_ref=dst, send_sem=send_sems.at[i], recv_sem=recv_sems.at[i],
                                            device_id=device, device_id_type=MESH)

    barrier = pltpu.get_barrier_semaphore()
    for i in range(1, n):
        pl.semaphore_signal(barrier, inc=1, device_id=peer(i)[1], device_id_type=MESH)

    spread_r, spread_c = iota((32, 256), 0), iota((32, 256), 1)
    spread = jnp.where((spread_c // 32 == spread_r // 4) & (spread_c % 4 == spread_r % 4), 1.0, 0.0).astype(BF16)
    lane_x = (iota((nz, 256), 1) // 4) % 8
    for ref, part in zip((bd_h, bd_l), split(fz[...])):
        wide = dot(part, spread)
        for j in range(8):
            ref[j * nz:(j + 1) * nz, :] = jnp.where(lane_x == j, wide, 0.0).astype(BF16)
    bd = (bd_h[...], bd_l[...])

    pl.semaphore_wait(barrier, n - 1)

    copies = []
    for i in range(1, nsx):
        copies.append(send(fx, ux.at[sx], ux_s, ux_r, i, {"sx": lax.rem(sx + i, nsx)}))
    for i in range(1, nsy):
        copies.append(send(fy, uy.at[sy], uy_s, uy_r, i, {"sy": lax.rem(sy + i, nsy)}))
    for copy in copies:
        copy.start()
    ux[pl.ds(sx, 1)] = fx[...][None]
    uy[pl.ds(sy, 1)] = fy[...][None]

    xo = xl // 8
    for s in range(snaps):
        snap = field[s].reshape(xo, 8, yl, nz)
        rows = jnp.concatenate([snap[:, j].reshape(xo * yl, nz) for j in range(8)], axis=1)
        packed = dot3(split(rows), bd)
        for t in range(2):
            tiles = [packed[o * yl:(o + 1) * yl, t * 128:(t + 1) * 128] for o in range(xo)]
            for k, tile in enumerate(exchange_segments(tiles)):
                send1[s * 8 + t * 4 + k] = tile

    first = []
    for i in range(1, n):
        q, device = peer(i)
        first.append(send(send1.at[q], recv1.at[me], s1_s, s1_r, i, device))
    for copy in first:
        copy.start()
    recv1[pl.ds(me, 1)] = send1[pl.ds(me, 1)]

    for copy in copies:
        copy.wait()
    uy_all = uy[...].reshape(nsy * yl, uy.shape[2])
    ux_all = ux[...].reshape(nsx * xl, ux.shape[2])
    rank1, rank2 = ux_all.shape[1], uy_all.shape[1]
    uy_p = split(uy_all)
    eye = jnp.where(iota((rank2, rank2), 0) == iota((rank2, rank2), 1), 1.0, 0.0).astype(BF16)
    left = jnp.concatenate([dot3(uy_p, uy_p, NT), dot(eye, uy_p[0], NT) + dot(eye, uy_p[1], NT)], axis=0)
    left = split(left)
    nx = nsx * xl
    wide_x = 4 * nx
    repeat = jnp.where(iota((wide_x, nx), 0) // 4 == iota((wide_x, nx), 1), 1.0, 0.0).astype(BF16)
    ux_pad = jnp.concatenate([ux_all, jnp.zeros((nx, 128 - rank1), F32)], axis=1)
    xe_f = [dot(repeat, part) for part in split(ux_pad)]
    xe = [part.astype(BF16) for part in xe_f]
    same = (iota((wide_x, wide_x), 0) % 4) == (iota((wide_x, wide_x), 1) % 4)
    px = split(jnp.where(same, dot3(xe, xe, NT), 0.0))
    row_c = iota((wide_x, 128), 0) % 4
    wx = [jnp.concatenate([jnp.where(row_c == c, part, 0.0).astype(BF16) for c in range(4)], axis=1) for part in xe_f]

    for copy in first:
        copy.wait()
    whole = jnp.concatenate([recv1[g * nsy:(g + 1) * nsy].reshape(nsy * yl, 128) for g in range(nsx)], axis=1)
    both = dot3(left, split(whole))
    back = dot3(split(both[:nsy * yl]), px)
    for g in range(nsx):
        send2[g * nsy:(g + 1) * nsy] = back[:, g * 128:(g + 1) * 128].reshape(nsy, yl, 128)
    second = []
    for i in range(1, n):
        q, device = peer(i)
        second.append(send(send2.at[q], recv2.at[me], s2_s, s2_r, i, device))
    for copy in second:
        copy.start()
    recv2[pl.ds(me, 1)] = send2[pl.ds(me, 1)]

    core = dot3(split(both[nsy * yl:]), wx)
    for q in range(n):
        for h in range(2):
            csend[q, h * 4:(h + 1) * 4, :] = core[q * 4:(q + 1) * 4, h * 256:(h + 1) * 256]
    third = []
    for i in range(1, n):
        q, device = peer(i)
        third.append(send(csend.at[q], crecv.at[me], c_s, c_r, i, device))
    for copy in third:
        copy.start()
    crecv[pl.ds(me, 1)] = csend[pl.ds(me, 1)]

    for copy in second:
        copy.wait()
    for s in range(snaps):
        halves = []
        for t in range(2):
            tiles = exchange_segments([recv2[s * 8 + t * 4 + k] for k in range(4)])
            halves.append(jnp.concatenate(tiles, axis=0))
        rebuilt = dot3(split(jnp.concatenate(halves, axis=1)), bd, NT)
        for j in range(8):
            for o in range(xo):
                res_out[s, o * 8 + j] = field[s, o * 8 + j] - rebuilt[o * yl:(o + 1) * yl, j * nz:(j + 1) * nz]

    for copy in third:
        copy.wait()
    k = iota((128, 128), 0)
    lane = (k % 4) * 32 + ((k // 8) % 8) * 4 + ((k // 4) % 2) * 2 + k // 64
    order = jnp.where(lane == iota((128, 128), 1), 1.0, 0.0).astype(BF16)
    for s in range(snaps):
        got = crecv[s * 8:(s + 1) * 8].reshape(64, 256)
        high, low = split(jnp.concatenate([got[:, :128], got[:, 128:]], axis=0))
        core_out[s] = (dot(high, order, TN) + dot(low, order, TN))[:rank1]


def plain(field, factor_x, factor_y, factor_z):
    highest = lax.Precision.HIGHEST
    inner = jnp.einsum("sxyz,zc->sxyc", field, factor_z, precision=highest)
    inner = jnp.einsum("sxyc,yb->sxbc", inner, factor_y, precision=highest)
    snaps = inner.shape[0]
    rank_one = factor_x.shape[1]
    rank_two = inner.shape[2]
    rank_three = inner.shape[3]
    flat_width = rank_two * rank_three
    partial_core = jnp.einsum("sxbc,xa->sabc", inner, factor_x, precision=highest)
    flat_terms = partial_core.reshape(snaps, rank_one, flat_width)
    core_slice = lax.psum_scatter(flat_terms, ("sx", "sy"), scatter_dimension=2, tiled=True)
    whole_core = lax.all_gather(core_slice, ("sx", "sy"), axis=2, tiled=True)
    kernel = whole_core.reshape(snaps, rank_one, rank_two, rank_three)
    outer = jnp.einsum("sabc,xa->sxbc", kernel, factor_x, precision=highest)
    outer = jnp.einsum("sxbc,yb->sxyc", outer, factor_y, precision=highest)
    outer = jnp.einsum("sxyc,zc->sxyz", outer, factor_z, precision=highest)
    return (core_slice, field - outer)


def local(nsx, nsy, field, factor_x, factor_y, factor_z):
    snaps, xl, yl, nz = field.shape
    rank1, rank2, rank3 = factor_x.shape[1], factor_y.shape[1], factor_z.shape[1]
    n = nsx * nsy
    fits = (n == 16 and snaps == 2 and rank3 == 32 and xl == 32 and nz == 128 and yl % 24 == 0 and rank2 == 64
            and rank1 <= 128 and rank1 % 8 == 0 and yl <= 64)
    if not fits:
        return plain(field, factor_x, factor_y, factor_z)
    vmem = pl.BlockSpec(memory_space=pltpu.VMEM)
    dma = pltpu.SemaphoreType.DMA
    return pl.pallas_call(
        functools.partial(kernel, nsx, nsy),
        out_shape=(jax.ShapeDtypeStruct((snaps, rank1, rank2 * rank3 // n), F32), jax.ShapeDtypeStruct(field.shape, F32)),
        in_specs=[vmem] * 4,
        out_specs=(vmem, vmem),
        scratch_shapes=[
            pltpu.VMEM((nsx, xl, rank1), F32),
            pltpu.VMEM((nsy, yl, rank2), F32),
            pltpu.VMEM((8 * nz, 256), BF16),
            pltpu.VMEM((8 * nz, 256), BF16),
            pltpu.VMEM((n, yl, 128), F32),
            pltpu.VMEM((n, yl, 128), F32),
            pltpu.VMEM((n, yl, 128), F32),
            pltpu.VMEM((n, yl, 128), F32),
            pltpu.VMEM((n, 8, 256), F32),
            pltpu.VMEM((n, 8, 256), F32),
            dma((nsx,)), dma((nsx,)), dma((nsy,)), dma((nsy,)),
            dma((n,)), dma((n,)), dma((n,)), dma((n,)), dma((n,)), dma((n,)),
        ],
        compiler_params=pltpu.CompilerParams(collective_id=0, has_side_effects=True, vmem_limit_bytes=40 * 2**20),
    )(field, factor_x, factor_y, factor_z)


def solution(mesh):
    in_specs = (P("grp", "sx", "sy", None), P("sx", None), P("sy", None), P())
    out_specs = (P("grp", None, ("sx", "sy")), P("grp", "sx", "sy", None))
    body = functools.partial(local, mesh.shape["sx"], mesh.shape["sy"])
    return jax.shard_map(body, mesh=mesh, in_specs=in_specs, out_specs=out_specs, check_vma=False)
```

```python
import functools

import jax
import jax.numpy as jnp
from jax import lax
from jax.experimental import pallas as pl
from jax.experimental.pallas import tpu as pltpu
from jax.sharding import PartitionSpec as P

STOP = 0
LIMIT = 40
MESH = pl.DeviceIdType.MESH
F32 = jnp.float32
BF16 = jnp.bfloat16
NN = (((1,), (0,)), ((), ()))
NT = (((1,), (1,)), ((), ()))
TN = (((0,), (0,)), ((), ()))


def split(a):
    high = a.astype(BF16)
    return high, (a - high.astype(F32)).astype(BF16)


def dot(a, b, dims=NN):
    return lax.dot_general(a, b, dims, preferred_element_type=F32)


def dot3(a, b, dims=NN):
    return dot(a[0], b[0], dims) + (dot(a[0], b[1], dims) + dot(a[1], b[0], dims))


def iota(shape, axis):
    return lax.broadcasted_iota(jnp.int32, shape, axis)


def exchange_segments(tiles):
    segment = iota(tiles[0].shape, 1) // 32
    a, b, c, d = tiles
    low = segment < 2
    a, c = jnp.where(low, a, pltpu.roll(c, 64, 1)), jnp.where(low, pltpu.roll(a, 64, 1), c)
    b, d = jnp.where(low, b, pltpu.roll(d, 64, 1)), jnp.where(low, pltpu.roll(b, 64, 1), d)
    even = segment % 2 == 0
    a, b = jnp.where(even, a, pltpu.roll(b, 32, 1)), jnp.where(even, pltpu.roll(a, 96, 1), b)
    c, d = jnp.where(even, c, pltpu.roll(d, 32, 1)), jnp.where(even, pltpu.roll(c, 96, 1), d)
    return a, b, c, d


def kernel(nsx, nsy, stop, field_hbm, fx, fy, fz_hbm, recv2, crecv, field, bd_h, bd_l, ux, uy, fz, send1, recv1, send2,
           csend, in_s, ux_s, ux_r, uy_s, uy_r, s1_s, s1_r, s2_s, s2_r, c_s, c_r):
    n = nsx * nsy
    snaps, xl, yl, nz = field.shape
    sx, sy = lax.axis_index("sx"), lax.axis_index("sy")
    me = sx * nsy + sy

    def peer(i):
        q = lax.rem(me + i, n)
        return q, {"sx": q // nsy, "sy": lax.rem(q, nsy)}

    def send(src, dst, send_sems, recv_sems, i, device):
        return pltpu.make_async_remote_copy(src_ref=src, dst_ref=dst, send_sem=send_sems.at[i], recv_sem=recv_sems.at[i],
                                            device_id=device, device_id_type=MESH)

    loads = [pltpu.make_async_copy(fz_hbm, fz, in_s.at[0])]
    for s in range(snaps):
        loads.append(pltpu.make_async_copy(field_hbm.at[s], field.at[s], in_s.at[1 + s]))
    loads.append(pltpu.make_async_copy(fx, ux.at[sx], in_s.at[1 + snaps]))
    loads.append(pltpu.make_async_copy(fy, uy.at[sy], in_s.at[2 + snaps]))
    for load in loads:
        load.start()

    barrier = pltpu.get_barrier_semaphore()
    for i in range(1, n):
        pl.semaphore_signal(barrier, inc=1, device_id=peer(i)[1], device_id_type=MESH)

    if stop == 7:
        pl.semaphore_wait(barrier, n - 1)
        for load in loads:
            load.wait()
        return
    spread_r, spread_c = iota((32, 256), 0), iota((32, 256), 1)
    spread = jnp.where((spread_c // 32 == spread_r // 4) & (spread_c % 4 == spread_r % 4), 1.0, 0.0).astype(BF16)
    loads[0].wait()
    lane_x = (iota((nz, 256), 1) // 4) % 8
    for ref, part in zip((bd_h, bd_l), split(fz[...])):
        wide = dot(part, spread, TN)
        for j in range(8):
            ref[j * nz:(j + 1) * nz, :] = jnp.where(lane_x == j, wide, 0.0).astype(BF16)
    bd = (bd_h[...], bd_l[...])

    pl.semaphore_wait(barrier, n - 1)

    if stop == 8:
        for load in loads[1:]:
            load.wait()
        return
    copies = []
    for i in range(1, nsx):
        copies.append(send(fx, ux.at[sx], ux_s, ux_r, i, {"sx": lax.rem(sx + i, nsx)}))
    for i in range(1, nsy):
        copies.append(send(fy, uy.at[sy], uy_s, uy_r, i, {"sy": lax.rem(sy + i, nsy)}))
    for copy in copies:
        copy.start()
    if stop == 1:
        for copy in copies + loads[1:]:
            copy.wait()
        return

    xo = xl // 8
    for s in range(snaps):
        loads[1 + s].wait()
        snap = field[s].reshape(xo, 8, yl, nz)
        rows = jnp.concatenate([snap[:, j].reshape(xo * yl, nz) for j in range(8)], axis=1)
        packed = dot3(split(rows), bd)
        for t in range(2):
            tiles = [packed[o * yl:(o + 1) * yl, t * 128:(t + 1) * 128] for o in range(xo)]
            for k, tile in enumerate(exchange_segments(tiles)):
                send1[s * 8 + t * 4 + k] = tile

    if stop == 2:
        for copy in copies + loads[1 + snaps:]:
            copy.wait()
        return
    first = []
    for i in range(1, n):
        q, device = peer(i)
        first.append(send(send1.at[q], recv1.at[me], s1_s, s1_r, i, device))
    for copy in first:
        copy.start()
    recv1[pl.ds(me, 1)] = send1[pl.ds(me, 1)]

    if stop == 3:
        for copy in copies + loads[1 + snaps:] + first:
            copy.wait()
        return
    for copy in copies + loads[1 + snaps:]:
        copy.wait()
    uy_all = uy[...].reshape(nsy * yl, uy.shape[2])
    ux_all = ux[...].reshape(nsx * xl, ux.shape[2])
    rank1, rank2 = ux_all.shape[1], uy_all.shape[1]
    uy_p = split(uy_all)
    eye = jnp.where(iota((rank2, rank2), 0) == iota((rank2, rank2), 1), 1.0, 0.0).astype(BF16)
    left = jnp.concatenate([dot3(uy_p, uy_p, NT), dot(eye, uy_p[0], NT) + dot(eye, uy_p[1], NT)], axis=0)
    left = split(left)
    nx = nsx * xl
    wide_x = 4 * nx
    repeat = jnp.where(iota((wide_x, nx), 0) // 4 == iota((wide_x, nx), 1), 1.0, 0.0).astype(BF16)
    ux_pad = jnp.concatenate([ux_all, jnp.zeros((nx, 128 - rank1), F32)], axis=1)
    xe_f = [dot(repeat, part) for part in split(ux_pad)]
    xe = [part.astype(BF16) for part in xe_f]
    same = (iota((wide_x, wide_x), 0) % 4) == (iota((wide_x, wide_x), 1) % 4)
    px = split(jnp.where(same, dot3(xe, xe, NT), 0.0))
    row_c = iota((wide_x, 128), 0) % 4
    wx = [jnp.concatenate([jnp.where(row_c == c, part, 0.0).astype(BF16) for c in range(4)], axis=1) for part in xe_f]

    for copy in first:
        copy.wait()
    if stop == 4:
        ux[0:1, :, :] = (px[0][:32, :96].astype(F32) + wx[0][:32, :96].astype(F32) + left[0][:32, :96].astype(F32))[None]
        return
    whole = jnp.concatenate([recv1[g * nsy:(g + 1) * nsy].reshape(nsy * yl, 128) for g in range(nsx)], axis=1)
    both = dot3(left, split(whole))
    back = dot3(split(both[:nsy * yl]), px)
    for g in range(nsx):
        send2[g * nsy:(g + 1) * nsy] = back[:, g * 128:(g + 1) * 128].reshape(nsy, yl, 128)
    if stop == 5:
        return
    second = []
    for i in range(1, n):
        q, device = peer(i)
        second.append(send(send2.at[q], recv2.at[me], s2_s, s2_r, i, device))
    for copy in second:
        copy.start()
    recv2[pl.ds(me, 1)] = send2[pl.ds(me, 1)]

    if stop == 6:
        for copy in second:
            copy.wait()
        return
    core = dot3(split(both[nsy * yl:]), wx)
    for q in range(n):
        for h in range(2):
            csend[q, h * 4:(h + 1) * 4, :] = core[q * 4:(q + 1) * 4, h * 256:(h + 1) * 256]
    third = []
    for i in range(1, n):
        q, device = peer(i)
        third.append(send(csend.at[q], crecv.at[me], c_s, c_r, i, device))
    for copy in third:
        copy.start()
    crecv[pl.ds(me, 1)] = csend[pl.ds(me, 1)]

    for copy in second + third:
        copy.wait()


def finish(recv2, crecv, field, bd_h, bd_l, core_hbm, res_hbm, core_out, res_out, sems):
    snaps, xl, yl, nz = field.shape
    rank1 = core_out.shape[1]
    xo = xl // 8
    bd = (bd_h[...], bd_l[...])
    stores = []
    for s in range(snaps):
        halves = []
        for t in range(2):
            tiles = exchange_segments([recv2[s * 8 + t * 4 + k] for k in range(4)])
            halves.append(jnp.concatenate(tiles, axis=0))
        rebuilt = dot3(split(jnp.concatenate(halves, axis=1)), bd, NT)
        for j in range(8):
            for o in range(xo):
                res_out[s, o * 8 + j] = field[s, o * 8 + j] - rebuilt[o * yl:(o + 1) * yl, j * nz:(j + 1) * nz]
        stores.append(pltpu.make_async_copy(res_out.at[s], res_hbm.at[s], sems.at[s]))
        stores[-1].start()

    k = iota((128, 128), 0)
    lane = (k % 4) * 32 + ((k // 8) % 8) * 4 + ((k // 4) % 2) * 2 + k // 64
    order = jnp.where(lane == iota((128, 128), 1), 1.0, 0.0).astype(BF16)
    for s in range(snaps):
        got = crecv[s * 8:(s + 1) * 8].reshape(64, 256)
        high, low = split(jnp.concatenate([got[:, :128], got[:, 128:]], axis=0))
        core_out[s] = (dot(high, order, TN) + dot(low, order, TN))[:rank1]
    stores.append(pltpu.make_async_copy(core_out, core_hbm, sems.at[snaps]))
    stores[-1].start()
    for store in stores:
        store.wait()


def plain(field, factor_x, factor_y, factor_z):
    highest = lax.Precision.HIGHEST
    inner = jnp.einsum("sxyz,zc->sxyc", field, factor_z, precision=highest)
    inner = jnp.einsum("sxyc,yb->sxbc", inner, factor_y, precision=highest)
    snaps = inner.shape[0]
    rank_one = factor_x.shape[1]
    rank_two = inner.shape[2]
    rank_three = inner.shape[3]
    flat_width = rank_two * rank_three
    partial_core = jnp.einsum("sxbc,xa->sabc", inner, factor_x, precision=highest)
    flat_terms = partial_core.reshape(snaps, rank_one, flat_width)
    core_slice = lax.psum_scatter(flat_terms, ("sx", "sy"), scatter_dimension=2, tiled=True)
    whole_core = lax.all_gather(core_slice, ("sx", "sy"), axis=2, tiled=True)
    kernel = whole_core.reshape(snaps, rank_one, rank_two, rank_three)
    outer = jnp.einsum("sabc,xa->sxbc", kernel, factor_x, precision=highest)
    outer = jnp.einsum("sxbc,yb->sxyc", outer, factor_y, precision=highest)
    outer = jnp.einsum("sxyc,zc->sxyz", outer, factor_z, precision=highest)
    return (core_slice, field - outer)


def local(nsx, nsy, field, factor_x, factor_y, factor_z):
    snaps, xl, yl, nz = field.shape
    rank1, rank2, rank3 = factor_x.shape[1], factor_y.shape[1], factor_z.shape[1]
    n = nsx * nsy
    fits = (n == 16 and snaps == 2 and rank3 == 32 and xl == 32 and nz == 128 and yl % 24 == 0 and rank2 == 64
            and rank1 <= 128 and rank1 % 8 == 0 and yl <= 64)
    if not fits:
        return plain(field, factor_x, factor_y, factor_z)
    vmem = pl.BlockSpec(memory_space=pltpu.VMEM)
    dma = pltpu.SemaphoreType.DMA
    hbm = pl.BlockSpec(memory_space=pltpu.HBM)
    wide = (n, yl, 128)
    passed = pl.pallas_call(
        functools.partial(kernel, nsx, nsy, STOP),
        out_shape=(
            jax.ShapeDtypeStruct(wide, F32),
            jax.ShapeDtypeStruct((n, 8, 256), F32),
            jax.ShapeDtypeStruct(field.shape, F32),
            jax.ShapeDtypeStruct((8 * nz, 256), BF16),
            jax.ShapeDtypeStruct((8 * nz, 256), BF16),
        ),
        in_specs=[hbm] * 4,
        out_specs=(vmem,) * 5,
        scratch_shapes=[
            pltpu.VMEM((nsx, xl, rank1), F32),
            pltpu.VMEM((nsy, yl, rank2), F32),
            pltpu.VMEM((rank3, nz), F32),
            pltpu.VMEM(wide, F32),
            pltpu.VMEM(wide, F32),
            pltpu.VMEM(wide, F32),
            pltpu.VMEM((n, 8, 256), F32),
            dma((snaps + 3,)),
            dma((nsx,)), dma((nsx,)), dma((nsy,)), dma((nsy,)),
            dma((n,)), dma((n,)), dma((n,)), dma((n,)), dma((n,)), dma((n,)),
        ],
        compiler_params=pltpu.CompilerParams(collective_id=0, has_side_effects=True, vmem_limit_bytes=LIMIT * 2**20),
    )(*[pltpu.with_memory_space_constraint(v, pltpu.HBM) for v in (field, factor_x, factor_y, factor_z.T)])
    core_shape = (snaps, rank1, rank2 * rank3 // n)
    return pl.pallas_call(
        finish,
        out_shape=(jax.ShapeDtypeStruct(core_shape, F32), jax.ShapeDtypeStruct(field.shape, F32)),
        in_specs=[vmem] * 5,
        out_specs=(hbm, hbm),
        scratch_shapes=[pltpu.VMEM(core_shape, F32), pltpu.VMEM(field.shape, F32), dma((snaps + 1,))],
        compiler_params=pltpu.CompilerParams(vmem_limit_bytes=40 * 2**20),
    )(*passed)


def solution(mesh):
    in_specs = (P("grp", "sx", "sy", None), P("sx", None), P("sy", None), P())
    out_specs = (P("grp", None, ("sx", "sy")), P("grp", "sx", "sy", None))
    body = functools.partial(local, mesh.shape["sx"], mesh.shape["sy"])
    return jax.shard_map(body, mesh=mesh, in_specs=in_specs, out_specs=out_specs, check_vma=False)
```

```python
import functools

import jax
import jax.numpy as jnp
from jax import lax
from jax.experimental import pallas as pl
from jax.experimental.pallas import tpu as pltpu
from jax.sharding import PartitionSpec as P

PARTS = 2
MESH = pl.DeviceIdType.MESH
F32 = jnp.float32
BF16 = jnp.bfloat16
NN = (((1,), (0,)), ((), ()))
NT = (((1,), (1,)), ((), ()))
TN = (((0,), (0,)), ((), ()))


def split(a):
    high = a.astype(BF16)
    return high, (a - high.astype(F32)).astype(BF16)


def dot(a, b, dims=NN):
    return lax.dot_general(a, b, dims, preferred_element_type=F32)


def dot3(a, b, dims=NN):
    return dot(a[0], b[0], dims) + (dot(a[0], b[1], dims) + dot(a[1], b[0], dims))


def iota(shape, axis):
    return lax.broadcasted_iota(jnp.int32, shape, axis)


def exchange_segments(tiles):
    segment = iota(tiles[0].shape, 1) // 32
    a, b, c, d = tiles
    low = segment < 2
    a, c = jnp.where(low, a, pltpu.roll(c, 64, 1)), jnp.where(low, pltpu.roll(a, 64, 1), c)
    b, d = jnp.where(low, b, pltpu.roll(d, 64, 1)), jnp.where(low, pltpu.roll(b, 64, 1), d)
    even = segment % 2 == 0
    a, b = jnp.where(even, a, pltpu.roll(b, 32, 1)), jnp.where(even, pltpu.roll(a, 96, 1), b)
    c, d = jnp.where(even, c, pltpu.roll(d, 32, 1)), jnp.where(even, pltpu.roll(c, 96, 1), d)
    return a, b, c, d


def kernel(nsx, nsy, parts, field_hbm, fx, fy, fz_hbm, recv2, crecv, field, bd_h, bd_l, ux, uy, fz, send1, recv1, bsend,
           brecv, rsend, rrecv, send2, csend, in_s, ux_s, ux_r, uy_s, uy_r, a1_s, a1_r, b1_s, b1_r, b2_s, b2_r, a2_s, a2_r,
           c_s, c_r):
    snaps, xl, yl, nz = field.shape
    cgs = send1.shape[1]
    each = cgs // parts
    bl = bsend.shape[2]
    sx, sy = lax.axis_index("sx"), lax.axis_index("sy")
    z_order, y_order = (2, 1, 3), (2, 1, 3)

    def to_x(i):
        q = lax.rem(sx + i, nsx)
        return q, {"sx": q}

    def to_y(i):
        q = lax.rem(sy + i, nsy)
        return q, {"sy": q}

    def send(src, dst, send_sem, recv_sem, device):
        return pltpu.make_async_remote_copy(src_ref=src, dst_ref=dst, send_sem=send_sem, recv_sem=recv_sem,
                                            device_id=device, device_id_type=MESH)

    def exchange(source, landing, me, peer_of, order, sems, p):
        started = []
        for i in order:
            q, device = peer_of(i)
            started.append(send(source.at[q, p * each:(p + 1) * each], landing.at[me, p * each:(p + 1) * each],
                                sems[0].at[p * 4 + i], sems[1].at[p * 4 + i], device))
            started[-1].start()
        landing[pl.ds(me, 1), p * each:(p + 1) * each] = source[pl.ds(me, 1), p * each:(p + 1) * each]
        return started

    def finish_all(started):
        for copy in started:
            copy.wait()

    loads = [pltpu.make_async_copy(fz_hbm, fz, in_s.at[0])]
    for s in range(snaps):
        loads.append(pltpu.make_async_copy(field_hbm.at[s], field.at[s], in_s.at[1 + s]))
    loads.append(pltpu.make_async_copy(fx, ux.at[sx], in_s.at[1 + snaps]))
    loads.append(pltpu.make_async_copy(fy, uy.at[sy], in_s.at[2 + snaps]))
    for load in loads:
        load.start()

    barrier = pltpu.get_barrier_semaphore()
    for i in z_order:
        pl.semaphore_signal(barrier, inc=1, device_id=to_x(i)[1], device_id_type=MESH)
    for i in y_order:
        pl.semaphore_signal(barrier, inc=1, device_id=to_y(i)[1], device_id_type=MESH)

    spread_r, spread_c = iota((32, 256), 0), iota((32, 256), 1)
    spread = jnp.where((spread_c // 32 == spread_r // 4) & (spread_c % 4 == spread_r % 4), 1.0, 0.0).astype(BF16)
    loads[0].wait()
    lane_x = (iota((nz, 256), 1) // 4) % 8
    for ref, part in zip((bd_h, bd_l), split(fz[...])):
        wide = dot(part, spread, TN)
        for j in range(8):
            ref[j * nz:(j + 1) * nz, :] = jnp.where(lane_x == j, wide, 0.0).astype(BF16)
    bd = (bd_h[...], bd_l[...])

    xo = xl // 8
    for s in range(snaps):
        loads[1 + s].wait()
        snap = field[s].reshape(xo, 8, yl, nz)
        rows = jnp.concatenate([snap[:, j].reshape(xo * yl, nz) for j in range(8)], axis=1)
        packed = dot3(split(rows), bd)
        for t in range(2):
            tiles = [packed[o * yl:(o + 1) * yl, t * 128:(t + 1) * 128] for o in range(xo)]
            for k, tile in enumerate(exchange_segments(tiles)):
                send1[s * 2 + t, k] = tile

    pl.semaphore_wait(barrier, nsx + nsy - 2)
    factor_y = [send(fy, uy.at[sy], uy_s.at[i], uy_r.at[i], to_y(i)[1]) for i in y_order]
    factor_x = [send(fx, ux.at[sx], ux_s.at[i], ux_r.at[i], to_x(i)[1]) for i in z_order]
    for copy in factor_y:
        copy.start()
    a1 = [exchange(send1, recv1, sy, to_y, y_order, (a1_s, a1_r), p) for p in range(parts)]
    for copy in factor_x:
        copy.start()

    finish_all(loads[1 + snaps:] + factor_y)
    uy_all = uy[...].reshape(nsy * yl, uy.shape[2])
    rank2 = uy_all.shape[1]
    uy_p = split(uy_all)
    eye = jnp.where(iota((rank2, rank2), 0) == iota((rank2, rank2), 1), 1.0, 0.0).astype(BF16)
    uy_t = tuple(dot(eye, part, NT).astype(BF16) for part in uy_p)

    b1 = []
    for p in range(parts):
        finish_all(a1[p])
        mine = range(p * each, (p + 1) * each)
        h = jnp.concatenate([recv1[:, g].reshape(nsy * yl, 128) for g in mine], axis=1)
        z = dot3(uy_t, split(h))
        for k, g in enumerate(mine):
            bsend[:, g] = z[:, k * 128:(k + 1) * 128].reshape(nsx, bl, 128)
        b1.append(exchange(bsend, brecv, sx, to_x, z_order, (b1_s, b1_r), p))

    finish_all(factor_x)
    ux_all = ux[...].reshape(nsx * xl, ux.shape[2])
    rank1 = ux_all.shape[1]
    nx = nsx * xl
    wide_x = 4 * nx
    repeat = jnp.where(iota((wide_x, nx), 0) // 4 == iota((wide_x, nx), 1), 1.0, 0.0).astype(BF16)
    ux_pad = jnp.concatenate([ux_all, jnp.zeros((nx, 128 - rank1), F32)], axis=1)
    xe_f = [dot(repeat, part) for part in split(ux_pad)]
    xe = [part.astype(BF16) for part in xe_f]
    same = (iota((wide_x, wide_x), 0) % 4) == (iota((wide_x, wide_x), 1) % 4)
    px = split(jnp.where(same, dot3(xe, xe, NT), 0.0))
    row_c = iota((wide_x, 128), 0) % 4
    wx = [jnp.concatenate([jnp.where(row_c == c, part, 0.0).astype(BF16) for c in range(4)], axis=1) for part in xe_f]

    b2, got = [], []
    for p in range(parts):
        finish_all(b1[p])
        mine = range(p * each, (p + 1) * each)
        got.append(split(jnp.concatenate(
            [brecv[x, p * each:(p + 1) * each].reshape(each * bl, 128) for x in range(nsx)], axis=1)))
        r = dot3(got[p], px)
        for x in range(nsx):
            rsend[x, p * each:(p + 1) * each] = r[:, x * 128:(x + 1) * 128].reshape(each, bl, 128)
        b2.append(exchange(rsend, rrecv, sx, to_x, z_order, (b2_s, b2_r), p))

    third = []
    for p in range(parts):
        core = dot3(got[p], wx)
        for k in range(each):
            g = p * each + k
            for y in range(nsy):
                csend[y, g * 4:(g + 1) * 4, :] = core[k * bl + y * 4:k * bl + (y + 1) * 4, :]
    for i in y_order:
        q, device = to_y(i)
        third.append(send(csend.at[q], crecv.at[sy], c_s.at[i], c_r.at[i], device))
        third[-1].start()
    crecv[pl.ds(sy, 1)] = csend[pl.ds(sy, 1)]

    a2 = []
    for p in range(parts):
        finish_all(b2[p])
        mine = range(p * each, (p + 1) * each)
        r = jnp.concatenate([rrecv[:, g].reshape(rank2, 128) for g in mine], axis=1)
        y = dot3(uy_p, split(r))
        for k, g in enumerate(mine):
            send2[:, g] = y[:, k * 128:(k + 1) * 128].reshape(nsy, yl, 128)
        a2.append(exchange(send2, recv2, sy, to_y, y_order, (a2_s, a2_r), p))
    for started in a2 + [third]:
        finish_all(started)


def finish(recv2, crecv, field, bd_h, bd_l, core_hbm, res_hbm, core_out, res_out, sems):
    snaps, xl, yl, nz = field.shape
    rank1 = core_out.shape[1]
    xo = xl // 8
    bd = (bd_h[...], bd_l[...])
    stores = []
    for s in range(snaps):
        halves = []
        for t in range(2):
            tiles = exchange_segments([recv2[s * 2 + t, k] for k in range(4)])
            halves.append(jnp.concatenate(tiles, axis=0))
        rebuilt = dot3(split(jnp.concatenate(halves, axis=1)), bd, NT)
        for j in range(8):
            for o in range(xo):
                res_out[s, o * 8 + j] = field[s, o * 8 + j] - rebuilt[o * yl:(o + 1) * yl, j * nz:(j + 1) * nz]
        stores.append(pltpu.make_async_copy(res_out.at[s], res_hbm.at[s], sems.at[s]))
        stores[-1].start()

    k = iota((128, 128), 0)
    lane = (k % 4) * 32 + ((k // 4) % 8) * 4 + k // 32
    order = jnp.where(lane == iota((128, 128), 1), 1.0, 0.0).astype(BF16)
    for s in range(snaps):
        got = crecv[s * 2:(s + 1) * 2].reshape(32, 512)
        high, low = split(jnp.concatenate([got[:, c * 128:(c + 1) * 128] for c in range(4)], axis=0))
        core_out[s] = (dot(high, order, TN) + dot(low, order, TN))[:rank1]
    stores.append(pltpu.make_async_copy(core_out, core_hbm, sems.at[snaps]))
    stores[-1].start()
    for store in stores:
        store.wait()


def plain(field, factor_x, factor_y, factor_z):
    highest = lax.Precision.HIGHEST
    inner = jnp.einsum("sxyz,zc->sxyc", field, factor_z, precision=highest)
    inner = jnp.einsum("sxyc,yb->sxbc", inner, factor_y, precision=highest)
    snaps = inner.shape[0]
    rank_one = factor_x.shape[1]
    rank_two = inner.shape[2]
    rank_three = inner.shape[3]
    flat_width = rank_two * rank_three
    partial_core = jnp.einsum("sxbc,xa->sabc", inner, factor_x, precision=highest)
    flat_terms = partial_core.reshape(snaps, rank_one, flat_width)
    core_slice = lax.psum_scatter(flat_terms, ("sx", "sy"), scatter_dimension=2, tiled=True)
    whole_core = lax.all_gather(core_slice, ("sx", "sy"), axis=2, tiled=True)
    kernel = whole_core.reshape(snaps, rank_one, rank_two, rank_three)
    outer = jnp.einsum("sabc,xa->sxbc", kernel, factor_x, precision=highest)
    outer = jnp.einsum("sxbc,yb->sxyc", outer, factor_y, precision=highest)
    outer = jnp.einsum("sxyc,zc->sxyz", outer, factor_z, precision=highest)
    return (core_slice, field - outer)


def local(nsx, nsy, field, factor_x, factor_y, factor_z):
    snaps, xl, yl, nz = field.shape
    rank1, rank2, rank3 = factor_x.shape[1], factor_y.shape[1], factor_z.shape[1]
    n = nsx * nsy
    fits = (nsx == 4 and nsy == 4 and snaps == 2 and rank3 == 32 and xl == 32 and nz == 128 and yl % 24 == 0 and rank2 == 64
            and rank1 <= 128 and rank1 % 8 == 0 and yl <= 64)
    if not fits:
        return plain(field, factor_x, factor_y, factor_z)
    vmem = pl.BlockSpec(memory_space=pltpu.VMEM)
    dma = pltpu.SemaphoreType.DMA
    hbm = pl.BlockSpec(memory_space=pltpu.HBM)
    bl = rank2 // nsx
    a_shape, b_shape, c_shape = (nsy, 4, yl, 128), (nsx, 4, bl, 128), (nsy, 4 * rank2 // n, 512)
    passed = pl.pallas_call(
        functools.partial(kernel, nsx, nsy, PARTS),
        out_shape=(
            jax.ShapeDtypeStruct(a_shape, F32),
            jax.ShapeDtypeStruct(c_shape, F32),
            jax.ShapeDtypeStruct(field.shape, F32),
            jax.ShapeDtypeStruct((8 * nz, 256), BF16),
            jax.ShapeDtypeStruct((8 * nz, 256), BF16),
        ),
        in_specs=[hbm] * 4,
        out_specs=(vmem,) * 5,
        scratch_shapes=[
            pltpu.VMEM((nsx, xl, rank1), F32),
            pltpu.VMEM((nsy, yl, rank2), F32),
            pltpu.VMEM((rank3, nz), F32),
            pltpu.VMEM(a_shape, F32), pltpu.VMEM(a_shape, F32),
            pltpu.VMEM(b_shape, F32), pltpu.VMEM(b_shape, F32),
            pltpu.VMEM(b_shape, F32), pltpu.VMEM(b_shape, F32),
            pltpu.VMEM(a_shape, F32),
            pltpu.VMEM(c_shape, F32),
            dma((snaps + 3,)),
            dma((4,)), dma((4,)), dma((4,)), dma((4,)),
            dma((4 * PARTS,)), dma((4 * PARTS,)), dma((4 * PARTS,)), dma((4 * PARTS,)),
            dma((4 * PARTS,)), dma((4 * PARTS,)), dma((4 * PARTS,)), dma((4 * PARTS,)),
            dma((4,)), dma((4,)),
        ],
        compiler_params=pltpu.CompilerParams(collective_id=0, has_side_effects=True, vmem_limit_bytes=40 * 2**20),
    )(*[pltpu.with_memory_space_constraint(v, pltpu.HBM) for v in (field, factor_x, factor_y, factor_z.T)])
    core_shape = (snaps, rank1, rank2 * rank3 // n)
    return pl.pallas_call(
        finish,
        out_shape=(jax.ShapeDtypeStruct(core_shape, F32), jax.ShapeDtypeStruct(field.shape, F32)),
        in_specs=[vmem] * 5,
        out_specs=(hbm, hbm),
        scratch_shapes=[pltpu.VMEM(core_shape, F32), pltpu.VMEM(field.shape, F32), dma((snaps + 1,))],
        compiler_params=pltpu.CompilerParams(vmem_limit_bytes=40 * 2**20),
    )(*passed)


def solution(mesh):
    in_specs = (P("grp", "sx", "sy", None), P("sx", None), P("sy", None), P())
    out_specs = (P("grp", None, ("sx", "sy")), P("grp", "sx", "sy", None))
    body = functools.partial(local, mesh.shape["sx"], mesh.shape["sy"])
    return jax.shard_map(body, mesh=mesh, in_specs=in_specs, out_specs=out_specs, check_vma=False)
```

```python
import functools

import jax
import jax.numpy as jnp
from jax import lax
from jax.experimental import pallas as pl
from jax.experimental.pallas import tpu as pltpu
from jax.sharding import PartitionSpec as P

PARTS = 2
MESH = pl.DeviceIdType.MESH
F32 = jnp.float32
BF16 = jnp.bfloat16
NN = (((1,), (0,)), ((), ()))
NT = (((1,), (1,)), ((), ()))
TN = (((0,), (0,)), ((), ()))


def split(a):
    high = a.astype(BF16)
    return high, (a - high.astype(F32)).astype(BF16)


def dot(a, b, dims=NN):
    return lax.dot_general(a, b, dims, preferred_element_type=F32)


def dot3(a, b, dims=NN):
    return dot(a[0], b[0], dims) + (dot(a[0], b[1], dims) + dot(a[1], b[0], dims))


def iota(shape, axis):
    return lax.broadcasted_iota(jnp.int32, shape, axis)


def exchange_segments(tiles):
    segment = iota(tiles[0].shape, 1) // 32
    a, b, c, d = tiles
    low = segment < 2
    a, c = jnp.where(low, a, pltpu.roll(c, 64, 1)), jnp.where(low, pltpu.roll(a, 64, 1), c)
    b, d = jnp.where(low, b, pltpu.roll(d, 64, 1)), jnp.where(low, pltpu.roll(b, 64, 1), d)
    even = segment % 2 == 0
    a, b = jnp.where(even, a, pltpu.roll(b, 32, 1)), jnp.where(even, pltpu.roll(a, 96, 1), b)
    c, d = jnp.where(even, c, pltpu.roll(d, 32, 1)), jnp.where(even, pltpu.roll(c, 96, 1), d)
    return a, b, c, d


def kernel(nsx, nsy, parts, field_hbm, fx, fy, fz_hbm, recv2, crecv, field, bt_h, bt_l, ux, uy, fz, bd_h, bd_l, send1, recv1, bsend,
           brecv, rsend, rrecv, send2, csend, in_s, ux_s, ux_r, uy_s, uy_r, a1_s, a1_r, b1_s, b1_r, b2_s, b2_r, a2_s, a2_r,
           c_s, c_r):
    snaps, xl, yl, nz = field.shape
    cgs = send1.shape[1]
    each = cgs // parts
    bl = bsend.shape[2]
    sx, sy = lax.axis_index("sx"), lax.axis_index("sy")
    z_order, y_order = (2, 1, 3), (2, 1, 3)

    def to_x(i):
        q = lax.rem(sx + i, nsx)
        return q, {"sx": q}

    def to_y(i):
        q = lax.rem(sy + i, nsy)
        return q, {"sy": q}

    def send(src, dst, send_sem, recv_sem, device):
        return pltpu.make_async_remote_copy(src_ref=src, dst_ref=dst, send_sem=send_sem, recv_sem=recv_sem,
                                            device_id=device, device_id_type=MESH)

    def exchange(source, landing, axis, me, order, sems, p):
        for q in order:
            part = slice(p * each, (p + 1) * each)

            @pl.when(me != q)
            def _():
                send(source.at[q, part], landing.at[me, part], sems[0].at[p * 4 + q], sems[1].at[p * 4 + me], {axis: q}).start()

            @pl.when(me == q)
            def _():
                landing[q, part] = source[q, part]

    def arrived(source, landing, axis, me, sems, p):
        for q in range(4):
            part = slice(p * each, (p + 1) * each)

            @pl.when(me != q)
            def _():
                send(source.at[q, part], landing.at[q, part], sems[0].at[p * 4 + q], sems[1].at[p * 4 + q], {axis: q}).wait()

    def finish_all(started):
        for copy in started:
            copy.wait()

    loads = [pltpu.make_async_copy(fz_hbm, fz, in_s.at[0])]
    for s in range(snaps):
        loads.append(pltpu.make_async_copy(field_hbm.at[s], field.at[s], in_s.at[1 + s]))
    loads.append(pltpu.make_async_copy(fx, ux.at[sx], in_s.at[1 + snaps]))
    loads.append(pltpu.make_async_copy(fy, uy.at[sy], in_s.at[2 + snaps]))
    for load in loads:
        load.start()

    barrier = pltpu.get_barrier_semaphore()
    for i in z_order:
        pl.semaphore_signal(barrier, inc=1, device_id=to_x(i)[1], device_id_type=MESH)
    for i in y_order:
        pl.semaphore_signal(barrier, inc=1, device_id=to_y(i)[1], device_id_type=MESH)

    spread_r, spread_c = iota((32, 256), 0), iota((32, 256), 1)
    spread = jnp.where((spread_c // 32 == spread_r // 4) & (spread_c % 4 == spread_r % 4), 1.0, 0.0).astype(BF16)
    loads[0].wait()
    lane_x = (iota((nz, 256), 1) // 4) % 8
    for ref, part in zip((bd_h, bd_l), split(fz[...])):
        wide = dot(part, spread, TN)
        for j in range(8):
            ref[j * nz:(j + 1) * nz, :] = jnp.where(lane_x == j, wide, 0.0).astype(BF16)
    bd = (bd_h[...], bd_l[...])

    factor_y = [send(fy, uy.at[sy], uy_s.at[i], uy_r.at[i], to_y(i)[1]) for i in y_order]
    factor_x = [send(fx, ux.at[sx], ux_s.at[i], ux_r.at[i], to_x(i)[1]) for i in z_order]
    a1 = (send1, recv1, "sy", sy)
    b1 = (bsend, brecv, "sx", sx)
    b2 = (rsend, rrecv, "sx", sx)
    a2 = (send2, recv2, "sy", sy)
    xo = xl // 8
    for s in range(snaps):
        loads[1 + s].wait()
        snap = field[s].reshape(xo, 8, yl, nz)
        rows = jnp.concatenate([snap[:, j].reshape(xo * yl, nz) for j in range(8)], axis=1)
        packed = dot3(split(rows), bd)
        for t in range(2):
            tiles = [packed[o * yl:(o + 1) * yl, t * 128:(t + 1) * 128] for o in range(xo)]
            for k, tile in enumerate(exchange_segments(tiles)):
                send1[t * 2 + s, k] = tile
        if s == 0:
            pl.semaphore_wait(barrier, nsx + nsy - 2)
            for copy in factor_y:
                copy.start()
        for p in range(parts):
            exchange(*a1, (s, 2 + s), (a1_s, a1_r), p)
    for copy in factor_x:
        copy.start()

    spread_t = jnp.where((iota((256, 32), 0) // 32 == iota((256, 32), 1) // 4)
                         & (iota((256, 32), 0) % 4 == iota((256, 32), 1) % 4), 1.0, 0.0).astype(BF16)
    row_x = (iota((256, nz), 0) // 4) % 8
    for ref, part in zip((bt_h, bt_l), split(fz[...])):
        wide = dot(spread_t, part)
        for j in range(8):
            ref[:, j * nz:(j + 1) * nz] = jnp.where(row_x == j, wide, 0.0).astype(BF16)
    finish_all(loads[1 + snaps:] + factor_y)
    uy_all = uy[...].reshape(nsy * yl, uy.shape[2])
    rank2 = uy_all.shape[1]
    uy_p = split(uy_all)
    eye = jnp.where(iota((rank2, rank2), 0) == iota((rank2, rank2), 1), 1.0, 0.0).astype(BF16)
    uy_t = tuple(dot(eye, part, NT).astype(BF16) for part in uy_p)

    for p in range(parts):
        arrived(*a1, (a1_s, a1_r), p)
        mine = range(p * each, (p + 1) * each)
        h = jnp.concatenate([recv1[:, g].reshape(nsy * yl, 128) for g in mine], axis=1)
        z = dot3(uy_t, split(h))
        for k, g in enumerate(mine):
            bsend[:, g] = z[:, k * 128:(k + 1) * 128].reshape(nsx, bl, 128)
        exchange(*b1, (0, 1, 3, 2), (b1_s, b1_r), p)

    finish_all(factor_x)
    ux_all = ux[...].reshape(nsx * xl, ux.shape[2])
    rank1 = ux_all.shape[1]
    nx = nsx * xl
    wide_x = 4 * nx
    repeat = jnp.where(iota((wide_x, nx), 0) // 4 == iota((wide_x, nx), 1), 1.0, 0.0).astype(BF16)
    ux_pad = jnp.concatenate([ux_all, jnp.zeros((nx, 128 - rank1), F32)], axis=1)
    xe_f = [dot(repeat, part) for part in split(ux_pad)]
    xe = [part.astype(BF16) for part in xe_f]
    same = (iota((wide_x, wide_x), 0) % 4) == (iota((wide_x, wide_x), 1) % 4)
    px = split(jnp.where(same, dot3(xe, xe, NT), 0.0))
    row_c = iota((wide_x, 128), 0) % 4
    wx = [jnp.concatenate([jnp.where(row_c == c, part, 0.0).astype(BF16) for c in range(4)], axis=1) for part in xe_f]

    got = []
    for p in range(parts):
        arrived(*b1, (b1_s, b1_r), p)
        mine = range(p * each, (p + 1) * each)
        got.append(split(jnp.concatenate(
            [brecv[x, p * each:(p + 1) * each].reshape(each * bl, 128) for x in range(nsx)], axis=1)))
        r = dot3(got[p], px)
        for x in range(nsx):
            rsend[x, p * each:(p + 1) * each] = r[:, x * 128:(x + 1) * 128].reshape(each, bl, 128)
        exchange(*b2, (0, 1, 3, 2), (b2_s, b2_r), p)

    third = []
    for p in range(parts):
        core = dot3(got[p], wx)
        for k in range(each):
            g = p * each + k
            for y in range(nsy):
                csend[y, g * 4:(g + 1) * 4, :] = core[k * bl + y * 4:k * bl + (y + 1) * 4, :]
    for i in y_order:
        q, device = to_y(i)
        third.append(send(csend.at[q], crecv.at[sy], c_s.at[i], c_r.at[i], device))
        third[-1].start()
    crecv[pl.ds(sy, 1)] = csend[pl.ds(sy, 1)]

    for p in range(parts):
        arrived(*b2, (b2_s, b2_r), p)
        mine = range(p * each, (p + 1) * each)
        r = jnp.concatenate([rrecv[:, g].reshape(rank2, 128) for g in mine], axis=1)
        y = dot3(uy_p, split(r))
        for k, g in enumerate(mine):
            send2[:, g] = y[:, k * 128:(k + 1) * 128].reshape(nsy, yl, 128)
        exchange(*a2, (0, 1, 2, 3), (a2_s, a2_r), p)
    for p in range(parts):
        arrived(*a2, (a2_s, a2_r), p)
    finish_all(third)


def finish(recv2, crecv, field, bt_h, bt_l, core_hbm, res_hbm, core_out, res_out, sems):
    snaps, xl, yl, nz = field.shape
    rank1 = core_out.shape[1]
    xo = xl // 8
    bt = (bt_h[...], bt_l[...])
    stores = []
    for s in range(snaps):
        halves = []
        for t in range(2):
            tiles = exchange_segments([recv2[t * 2 + s, k] for k in range(4)])
            halves.append(jnp.concatenate(tiles, axis=0))
        rebuilt = dot3(split(jnp.concatenate(halves, axis=1)), bt)
        for j in range(8):
            for o in range(xo):
                res_out[s, o * 8 + j] = field[s, o * 8 + j] - rebuilt[o * yl:(o + 1) * yl, j * nz:(j + 1) * nz]
        stores.append(pltpu.make_async_copy(res_out.at[s], res_hbm.at[s], sems.at[s]))
        stores[-1].start()

    k = iota((128, 128), 0)
    lane = (k % 4) * 32 + ((k // 4) % 8) * 4 + k // 32
    order = jnp.where(lane == iota((128, 128), 1), 1.0, 0.0).astype(BF16)
    for s in range(snaps):
        got = jnp.concatenate([crecv[s], crecv[2 + s]], axis=0)
        high, low = split(jnp.concatenate([got[:, c * 128:(c + 1) * 128] for c in range(4)], axis=0))
        core_out[s] = (dot(high, order, TN) + dot(low, order, TN))[:rank1]
    stores.append(pltpu.make_async_copy(core_out, core_hbm, sems.at[snaps]))
    stores[-1].start()
    for store in stores:
        store.wait()


def plain(field, factor_x, factor_y, factor_z):
    highest = lax.Precision.HIGHEST
    inner = jnp.einsum("sxyz,zc->sxyc", field, factor_z, precision=highest)
    inner = jnp.einsum("sxyc,yb->sxbc", inner, factor_y, precision=highest)
    snaps = inner.shape[0]
    rank_one = factor_x.shape[1]
    rank_two = inner.shape[2]
    rank_three = inner.shape[3]
    flat_width = rank_two * rank_three
    partial_core = jnp.einsum("sxbc,xa->sabc", inner, factor_x, precision=highest)
    flat_terms = partial_core.reshape(snaps, rank_one, flat_width)
    core_slice = lax.psum_scatter(flat_terms, ("sx", "sy"), scatter_dimension=2, tiled=True)
    whole_core = lax.all_gather(core_slice, ("sx", "sy"), axis=2, tiled=True)
    kernel = whole_core.reshape(snaps, rank_one, rank_two, rank_three)
    outer = jnp.einsum("sabc,xa->sxbc", kernel, factor_x, precision=highest)
    outer = jnp.einsum("sxbc,yb->sxyc", outer, factor_y, precision=highest)
    outer = jnp.einsum("sxyc,zc->sxyz", outer, factor_z, precision=highest)
    return (core_slice, field - outer)


def local(nsx, nsy, field, factor_x, factor_y, factor_z):
    snaps, xl, yl, nz = field.shape
    rank1, rank2, rank3 = factor_x.shape[1], factor_y.shape[1], factor_z.shape[1]
    n = nsx * nsy
    fits = (nsx == 4 and nsy == 4 and snaps == 2 and rank3 == 32 and xl == 32 and nz == 128 and yl % 24 == 0 and rank2 == 64
            and rank1 <= 128 and rank1 % 8 == 0 and yl <= 64)
    if not fits:
        return plain(field, factor_x, factor_y, factor_z)
    vmem = pl.BlockSpec(memory_space=pltpu.VMEM)
    dma = pltpu.SemaphoreType.DMA
    hbm = pl.BlockSpec(memory_space=pltpu.HBM)
    bl = rank2 // nsx
    a_shape, b_shape, c_shape = (nsy, 4, yl, 128), (nsx, 4, bl, 128), (nsy, 4 * rank2 // n, 512)
    passed = pl.pallas_call(
        functools.partial(kernel, nsx, nsy, PARTS),
        out_shape=(
            jax.ShapeDtypeStruct(a_shape, F32),
            jax.ShapeDtypeStruct(c_shape, F32),
            jax.ShapeDtypeStruct(field.shape, F32),
            jax.ShapeDtypeStruct((256, 8 * nz), BF16),
            jax.ShapeDtypeStruct((256, 8 * nz), BF16),
        ),
        in_specs=[hbm] * 4,
        out_specs=(vmem,) * 5,
        scratch_shapes=[
            pltpu.VMEM((nsx, xl, rank1), F32),
            pltpu.VMEM((nsy, yl, rank2), F32),
            pltpu.VMEM((rank3, nz), F32),
            pltpu.VMEM((8 * nz, 256), BF16), pltpu.VMEM((8 * nz, 256), BF16),
            pltpu.VMEM(a_shape, F32), pltpu.VMEM(a_shape, F32),
            pltpu.VMEM(b_shape, F32), pltpu.VMEM(b_shape, F32),
            pltpu.VMEM(b_shape, F32), pltpu.VMEM(b_shape, F32),
            pltpu.VMEM(a_shape, F32),
            pltpu.VMEM(c_shape, F32),
            dma((snaps + 3,)),
            dma((4,)), dma((4,)), dma((4,)), dma((4,)),
            dma((4 * PARTS,)), dma((4 * PARTS,)), dma((4 * PARTS,)), dma((4 * PARTS,)),
            dma((4 * PARTS,)), dma((4 * PARTS,)), dma((4 * PARTS,)), dma((4 * PARTS,)),
            dma((4,)), dma((4,)),
        ],
        compiler_params=pltpu.CompilerParams(collective_id=0, has_side_effects=True, vmem_limit_bytes=40 * 2**20),
    )(*[pltpu.with_memory_space_constraint(v, pltpu.HBM) for v in (field, factor_x, factor_y, factor_z.T)])
    core_shape = (snaps, rank1, rank2 * rank3 // n)
    return pl.pallas_call(
        finish,
        out_shape=(jax.ShapeDtypeStruct(core_shape, F32), jax.ShapeDtypeStruct(field.shape, F32)),
        in_specs=[vmem] * 5,
        out_specs=(hbm, hbm),
        scratch_shapes=[pltpu.VMEM(core_shape, F32), pltpu.VMEM(field.shape, F32), dma((snaps + 1,))],
        compiler_params=pltpu.CompilerParams(vmem_limit_bytes=40 * 2**20),
    )(*passed)


def solution(mesh):
    in_specs = (P("grp", "sx", "sy", None), P("sx", None), P("sy", None), P())
    out_specs = (P("grp", None, ("sx", "sy")), P("grp", "sx", "sy", None))
    body = functools.partial(local, mesh.shape["sx"], mesh.shape["sy"])
    return jax.shard_map(body, mesh=mesh, in_specs=in_specs, out_specs=out_specs, check_vma=False)
```
